512 devices in a mesh: wide: 64 (over z, y_lo, core), narrow: 8 (over y_hi, x).
Axes of the slice: x: 4, y: 8 (y_hi: 2, y_lo: 4; y = y_hi * 4 + y_lo), z: 8, core: 2. Of those that a mesh axis runs over, the one named last changes fastest.
Arguments:
- member_weights: bfloat16 [8, 128, 128, 128], P('narrow', 'wide'), may hold values from -6 to 6
- perturbations: bfloat16 [8, 3, 128, 128, 128], P('narrow', None, 'wide'), may hold values from -2 to 2
- vertical: bfloat16 [3, 128, 128], replicated, may hold values from -1 to 2
- obs_column: int32 [131072], P('wide'), may hold values from 0 to 255
- obs_level: int32 [131072], P('wide'), may hold values from 0 to 127
- obs_count: int32 [64], P('wide'), may hold values from 512 to 2048, as said below
- quality_flag: int32 [131072], P('wide'), may hold values 0 or 1
- obs_value: float32 [3, 131072], P(None, 'wide'), may hold values from -6 to 6
- obs_weight: float32 [3, 131072], P(None, 'wide'), may hold values from 1 to 10
Outputs:
- gradient: float32 [8, 128, 128, 128], P('narrow', 'wide')
The draws below stay inside these ranges and needn't reach their ends.
Inputs may be any that keep to these rules, and one draw needn't show every extreme that they name: Each column block uses its first obs_count slots; at most 2048 observations a block, and some block holds exactly 2048.
All inputs are finite; a program needn't handle non-finite values. No bound on the sum of `quality_flag` on one device may be relied on, other than what follows from the above.
Results may differ from the reference program's by a relative error of at most 0.008.
Values may be sent and summed in bfloat16 or wider, within the bound.
A program may use at most 128 MiB of HBM per device.

```python
import math
import jax
import jax.numpy as jnp
from jax import lax

NX = 128
NY = 128
VARS = 3
OBS_DEV = 2048
MEMBERS = 8
NL = 128
ROWS = 2
COLS_DEV = 256
BLOCKS = 64
OBS = 131072


def draw_vertical(key, part):
    identity = jnp.eye(NL, dtype=jnp.float32)
    noise = jax.random.truncated_normal(key, -3.0, 3.0, (VARS, NL, NL), jnp.float32)
    return (identity[None] + 0.5 * noise / jnp.sqrt(jnp.float32(NL))).astype(jnp.bfloat16)


def draw_obs_count(key, part):
    key_counts = jax.random.fold_in(key, 11)
    key_full = jax.random.fold_in(key, 23)
    counts = jax.random.randint(key_counts, (BLOCKS,), OBS_DEV // 4, OBS_DEV + 1, dtype=jnp.int32)
    full_block = jax.random.randint(key_full, (), 0, BLOCKS, dtype=jnp.int32)
    return jnp.where(jnp.arange(BLOCKS) == full_block, OBS_DEV, counts).astype(jnp.int32)


def set_ends(drawn, rng, low, high):
    longest = drawn.shape.index(max(drawn.shape))
    spots = []
    for shift in (0, 1):
        where = [jax.random.randint(jax.random.fold_in(rng, axis), (), 0, length) for axis, length in enumerate(drawn.shape)]
        where[longest] = (where[longest] + shift) % drawn.shape[longest]
        spots.append(tuple(where))
    return drawn.at[spots[0]].set(low).at[spots[1]].set(high)


def block_scale(rng, dims, split, least, high):
    gain, own = 1.0, jax.random.fold_in(rng, 6)
    for dim, blocks in split:
        heights = jnp.exp(jax.random.uniform(jax.random.fold_in(own, dim), (blocks,), jnp.float32, least / len(split), high / len(split)))
        gain = gain * jnp.repeat(heights, dims[dim] // blocks).reshape([-1 if axis == dim else 1 for axis in range(len(dims))])
    return gain


def gaussian(rng, extent, scale, reach, pieces=(), held_as=jnp.bfloat16):
    entries = jax.random.normal(rng, extent, jnp.float32) * scale
    if len(pieces) > 0:
        entries = block_scale(rng, extent, pieces, -0.22, 0.18) * entries
    return jnp.clip(entries, min=-reach, max=reach).astype(held_as)


def setup_inputs(seed: int = 0) -> dict:
    key_list = jax.random.split(jax.random.key(seed), 10)
    return {
        "member_weights": gaussian(key_list[0], (MEMBERS, NL, NX, NY), 1.0, 6.0, ((0, 8), (1, 64))),
        "perturbations": gaussian(key_list[1], (MEMBERS, VARS, NX, NL, NY), MEMBERS ** -0.5, 2.0, ((0, 8), (2, 64))),
        "vertical": draw_vertical(jax.random.fold_in(key_list[9], 71), 0),
        "obs_column": set_ends(jax.random.randint(key_list[3], (OBS,), 0, COLS_DEV), jax.random.fold_in(key_list[3], 1), 0, COLS_DEV - 1).astype(jnp.int32),
        "obs_level": set_ends(jax.random.randint(key_list[4], (OBS,), 0, NL), jax.random.fold_in(key_list[4], 1), 0, NL - 1).astype(jnp.int32),
        "obs_count": draw_obs_count(jax.random.fold_in(key_list[9], 71), 0),
        "quality_flag": set_ends((jax.random.randint(key_list[6], (OBS,), 0, 4) < 3).astype(jnp.int32), jax.random.fold_in(key_list[6], 1), 0, 1),
        "obs_value": gaussian(key_list[7], (VARS, OBS), 1.0, 6.0, ((1, 64),), jnp.float32),
        "obs_weight": jnp.clip(jnp.exp(math.log(10.0) - 2.3025851 * jax.random.uniform(key_list[8], (VARS, OBS), jnp.float32) ** block_scale(key_list[8], (VARS, OBS), ((1, 64),), -0.2, 0.2)), 1.0, 10.0),
    }


scale_lengths = (1.5, 4.0, 12.0)
scale_mix = (0.6, 0.5, 0.4)

def gauss_table(length, spread):
    places = jnp.arange(length).astype(jnp.float32)
    offset = places[:, None] - places[None, :]
    norm_factor = jnp.sqrt(jnp.sqrt(jnp.float32(jnp.pi)) * spread)
    values = jnp.exp(-0.5 * offset * offset / (spread * spread)) / norm_factor
    values = jnp.where(jnp.abs(offset) <= 4.0 * spread, values, jnp.float32(0.0))
    return values.astype(jnp.bfloat16)

def reference(member_weights, perturbations, vertical, obs_column, obs_level, obs_count, quality_flag, obs_value, obs_weight):
    tables = [(gauss_table(NX, spread_len).astype(jnp.float32), gauss_table(NY, spread_len).astype(jnp.float32)) for spread_len in scale_lengths]
    vertical_wide = vertical.astype(jnp.float32)

    def localize(weights_one):
        weights_wide = weights_one.astype(jnp.float32)
        summed = jnp.zeros((NX, NL, NY), jnp.float32)
        for (table_x, table_y), mix in zip(tables, scale_mix):
            across = jnp.einsum('ix,lxy->liy', table_x, weights_wide).astype(jnp.bfloat16)
            summed = summed + mix * jnp.einsum('liy,yz->ilz', across.astype(jnp.float32), table_y)
        return summed.astype(jnp.bfloat16)

    def add_member(running, pair):
        weights_one, perturb_one = pair
        localized = localize(weights_one).astype(jnp.float32)
        return (running + perturb_one.astype(jnp.float32) * localized[None], None)
    member_total, unused = lax.scan(add_member, jnp.zeros((VARS, NX, NL, NY), jnp.float32), (member_weights, perturbations))
    total_low = member_total.astype(jnp.bfloat16).astype(jnp.float32)
    increment = jnp.einsum('vlk,vxky->vxly', vertical_wide, total_low)
    slots = jnp.arange(OBS).astype(jnp.int32)
    block_of = slots // OBS_DEV
    within = slots % OBS_DEV
    live = (within < obs_count[block_of]) & (quality_flag > 0)
    row_of = block_of * ROWS + obs_column // NY
    col_of = obs_column % NY
    at_obs = increment[:, row_of, obs_level, col_of]
    misfit = jnp.where(live[None, :], obs_weight * (at_obs - obs_value), jnp.float32(0.0))
    obs_adjoint = jnp.zeros((VARS, NX, NL, NY), jnp.float32).at[:, row_of, obs_level, col_of].add(misfit)
    obs_adjoint = obs_adjoint.astype(jnp.bfloat16).astype(jnp.float32)
    vertical_adjoint = jnp.einsum('vkl,vxky->vxly', vertical_wide, obs_adjoint).astype(jnp.bfloat16).astype(jnp.float32)

    def member_gradient(pair):
        weights_one, perturb_one = pair
        column_grad = lax.optimization_barrier(jnp.sum(perturb_one.astype(jnp.float32) * vertical_adjoint, axis=0)).astype(jnp.bfloat16).astype(jnp.float32)
        result = weights_one.astype(jnp.float32)
        for (table_x, table_y), mix in zip(tables, scale_mix):
            back = jnp.einsum('ilz,yz->ily', column_grad, table_y).astype(jnp.bfloat16).astype(jnp.float32)
            result = result + mix * jnp.einsum('ix,ily->lxy', table_x, back)
        return result
    return lax.map(member_gradient, (member_weights, perturbations))
```

```python
import functools

import jax
import jax.numpy as jnp
import ml_dtypes
import numpy as np
from jax import lax
from jax.experimental import pallas as pl
from jax.experimental.pallas import tpu as pltpu
from jax.sharding import PartitionSpec as P

MESH = pl.DeviceIdType.MESH
scale_lengths = (1.5, 4.0, 12.0)
scale_mix = (0.6, 0.5, 0.4)
bf16, f32 = jnp.bfloat16, jnp.float32


def gauss_table(length, spread):
    places = np.arange(length).astype(np.float32)
    offset = places[:, None] - places[None, :]
    norm_factor = np.sqrt(np.sqrt(np.float32(np.pi)) * np.float32(spread))
    values = np.exp(np.float32(-0.5) * offset * offset / np.float32(spread * spread)) / norm_factor
    values = np.where(np.abs(offset) <= 4.0 * spread, values, np.float32(0.0))
    return values.astype(ml_dtypes.bfloat16)


def row_table(table, blocks, levels):
    length = table.shape[0]
    rows = length // blocks
    wide = np.zeros((rows, blocks, levels, levels, length), ml_dtypes.bfloat16)
    by_row = table.reshape(blocks, rows, length).transpose(1, 0, 2)
    for level in range(levels):
        wide[:, :, level, level, :] = by_row
    return wide.reshape(rows * blocks * levels, levels * length)


def dot(a, b):
    return jnp.dot(a, b, preferred_element_type=f32)


def kernel(
    nw, nn,
    weights_ref, perturb_ref, vertical_ref, to_rows_ref, to_levels_ref, table_ref,
    column_ref, level_ref, count_ref, flag_ref, value_ref, weight_ref,
    out_ref,
    send_a, recv_a, at_mine, at_all, send_b, recv_b, pick, pick_t, spread, vertical_t,
    send_sem, recv_sem, at_send_sem, at_recv_sem,
):
    me = lax.axis_index("wide")
    member = lax.axis_index("narrow")
    rows, blocks, levels, width = send_a.shape
    num_vars, num_levels, _ = vertical_ref.shape
    slot_rows = column_ref.shape[0]
    slots = slot_rows * 128
    cells = rows * width

    barrier = pltpu.get_barrier_semaphore()

    def greet(k, carry):
        peer = lax.rem(me + k, nw)
        pl.semaphore_signal(barrier, inc=1, device_id={"wide": peer}, device_id_type=MESH)
        return carry

    lax.fori_loop(1, nw, greet, 0)
    for k in range(1, nn):
        pl.semaphore_signal(
            barrier, inc=1, device_id={"narrow": lax.rem(member + k, nn)}, device_id_type=MESH
        )

    def exchange(source, target, phase):
        own = pltpu.make_async_copy(source.at[:, me], target.at[:, me], recv_sem.at[phase])
        own.start()

        def put(k, carry):
            peer = lax.rem(me + k, nw)
            pltpu.make_async_remote_copy(
                src_ref=source.at[:, peer],
                dst_ref=target.at[:, me],
                send_sem=send_sem.at[phase],
                recv_sem=recv_sem.at[phase],
                device_id={"wide": peer},
                device_id_type=MESH,
            ).start()
            return carry

        lax.fori_loop(1, nw, put, 0)

    def arrived(target, phase):
        pltpu.make_async_copy(target, target, recv_sem.at[phase]).wait()

    def departed(source, phase):
        part = source.at[:, pl.ds(0, nw - 1)]
        pltpu.make_async_copy(part, part, send_sem.at[phase]).wait()

    own_weights = weights_ref[...]
    localized = None
    for s, mix in enumerate(scale_mix):
        across = dot(to_rows_ref[s], own_weights).astype(bf16)
        scaled = mix * dot(across, table_ref[s])
        localized = scaled if localized is None else localized + scaled
    send_a[...] = localized.astype(bf16).reshape(send_a.shape)
    pl.semaphore_wait(barrier, nw - 1 + nn - 1)
    exchange(send_a, recv_a, 0)

    cell_of = lax.broadcasted_iota(jnp.int32, (cells, 128), 0)
    cell_of_t = lax.broadcasted_iota(jnp.int32, (128, cells), 1)
    columns = column_ref[...]
    columns_t = jnp.transpose(columns)
    for r in range(slot_rows):
        part = slice(r * 128, (r + 1) * 128)
        pick[:, part] = jnp.where(cell_of == columns[r : r + 1, :], 1.0, 0.0).astype(bf16)
        pick_t[part, :] = jnp.where(cell_of_t == columns_t[:, r : r + 1], 1.0, 0.0).astype(bf16)
    for v in range(num_vars):
        vertical_t[v] = jnp.transpose(vertical_ref[v].astype(f32)).astype(bf16)

    arrived(recv_a, 0)
    held = [recv_a[i].reshape(num_levels, width).astype(f32) for i in range(rows)]
    increment = []
    for v in range(num_vars):
        product = jnp.concatenate(
            [(perturb_ref[v * rows + i].astype(f32) * held[i]).astype(bf16) for i in range(rows)], axis=1
        )
        increment.append(dot(vertical_ref[v], product).astype(bf16))
    increment = jnp.concatenate(increment, axis=0)

    step = 256
    level_of = lax.broadcasted_iota(jnp.int32, (num_levels, 128), 0)
    for t in range(slots // step):
        met = dot(increment, pick[:, t * step : (t + 1) * step])
        for h in range(step // 128):
            r = t * (step // 128) + h
            here = level_of == level_ref[r : r + 1, :]
            for v in range(num_vars):
                block = met[v * num_levels : (v + 1) * num_levels, h * 128 : (h + 1) * 128]
                summed = jnp.sum(jnp.where(here, block, 0.0), axis=0, keepdims=True)
                at_mine[v, r : r + 1, :] = summed.astype(bf16)

    copies = []
    for k in range(1, nn):
        peer = lax.rem(member + k, nn)
        copy = pltpu.make_async_remote_copy(
            src_ref=at_mine,
            dst_ref=at_all.at[member],
            send_sem=at_send_sem,
            recv_sem=at_recv_sem,
            device_id={"narrow": peer},
            device_id_type=MESH,
        )
        copy.start()
        copies.append(copy)
    own = pltpu.make_async_copy(at_mine, at_all.at[member], at_recv_sem)
    own.start()
    pltpu.make_async_copy(at_all, at_all, at_recv_sem).wait()

    slot_of = lax.broadcasted_iota(jnp.int32, (slot_rows, 128), 0) * 128 + lax.broadcasted_iota(
        jnp.int32, (slot_rows, 128), 1
    )
    live = (slot_of < count_ref[0]) & (flag_ref[...] > 0)
    for v in range(num_vars):
        at_obs = at_all[0, v].astype(f32)
        for k in range(1, nn):
            at_obs = at_obs + at_all[k, v].astype(f32)
        misfit = jnp.where(live, weight_ref[v] * (at_obs - value_ref[v]), 0.0)
        for r in range(slot_rows):
            here = level_of == level_ref[r : r + 1, :]
            spread[v * num_levels : (v + 1) * num_levels, r * 128 : (r + 1) * 128] = jnp.where(
                here, misfit[r : r + 1, :], 0.0
            ).astype(bf16)
    adjoint = dot(spread[...], pick_t[...]).astype(bf16)

    sums = [None] * rows
    for v in range(num_vars):
        lifted = dot(vertical_t[v], adjoint[v * num_levels : (v + 1) * num_levels]).astype(bf16).astype(f32)
        for i in range(rows):
            term = perturb_ref[v * rows + i].astype(f32) * lifted[:, i * width : (i + 1) * width]
            sums[i] = term if sums[i] is None else sums[i] + term
    for i in range(rows):
        send_b[i] = sums[i].astype(bf16).reshape(send_b.shape[1:])
    exchange(send_b, recv_b, 1)
    arrived(recv_b, 1)

    level_grad = recv_b[...].reshape(rows * blocks * levels, width)
    gradient = own_weights.astype(f32)
    for s, mix in enumerate(scale_mix):
        back = dot(level_grad, table_ref[s]).astype(bf16)
        gradient = gradient + mix * dot(to_levels_ref[s], back)
    out_ref[...] = gradient

    departed(send_a, 0)
    departed(send_b, 1)
    pltpu.make_async_copy(at_all.at[pl.ds(0, nn - 1)], at_all.at[pl.ds(0, nn - 1)], at_send_sem).wait()


def solution(mesh):
    nw, nn = mesh.shape["wide"], mesh.shape["narrow"]

    def local(weights, perturb, vertical, obs_column, obs_level, obs_count, flag, obs_value, obs_weight):
        _, levels, length, width = weights.shape
        _, num_vars, rows, num_levels, _ = perturb.shape
        slots = obs_column.shape[0]
        slot_rows = slots // 128
        tables = [gauss_table(length, spread) for spread in scale_lengths]
        to_rows = np.stack([row_table(table, nw, levels) for table in tables])
        to_levels = np.ascontiguousarray(to_rows.transpose(0, 2, 1))
        chunk = pltpu.VMEM((rows, nw, levels, width), bf16)
        vmem = pl.BlockSpec(memory_space=pltpu.VMEM)
        smem = pl.BlockSpec(memory_space=pltpu.SMEM)
        out = pl.pallas_call(
            functools.partial(kernel, nw, nn),
            out_shape=jax.ShapeDtypeStruct((levels * length, width), f32),
            in_specs=[vmem] * 8 + [smem] + [vmem] * 3,
            out_specs=vmem,
            scratch_shapes=[
                chunk,
                chunk,
                pltpu.VMEM((num_vars, slot_rows, 128), bf16),
                pltpu.VMEM((nn, num_vars, slot_rows, 128), bf16),
                chunk,
                chunk,
                pltpu.VMEM((rows * width, slots), bf16),
                pltpu.VMEM((slots, rows * width), bf16),
                pltpu.VMEM((num_vars * num_levels, slots), bf16),
                pltpu.VMEM((num_vars, num_levels, num_levels), bf16),
                pltpu.SemaphoreType.DMA((2,)),
                pltpu.SemaphoreType.DMA((2,)),
                pltpu.SemaphoreType.DMA,
                pltpu.SemaphoreType.DMA,
            ],
            compiler_params=pltpu.CompilerParams(
                collective_id=0, has_side_effects=True, vmem_limit_bytes=48 * 1024 * 1024
            ),
        )(
            weights.reshape(levels * length, width),
            perturb.reshape(num_vars * rows, num_levels, width),
            vertical,
            jnp.asarray(to_rows),
            jnp.asarray(to_levels),
            jnp.asarray(np.stack(tables)),
            obs_column.reshape(slot_rows, 128),
            obs_level.reshape(slot_rows, 128),
            obs_count,
            flag.reshape(slot_rows, 128),
            obs_value.reshape(num_vars, slot_rows, 128),
            obs_weight.reshape(num_vars, slot_rows, 128),
        )
        return out.reshape(weights.shape)

    placed = (
        P("narrow", "wide", None, None),
        P("narrow", None, "wide", None, None),
        P(),
        P("wide"),
        P("wide"),
        P("wide"),
        P("wide"),
        P(None, "wide"),
        P(None, "wide"),
    )
    return jax.shard_map(
        local,
        mesh=mesh,
        in_specs=placed,
        out_specs=P("narrow", "wide", None, None),
        check_vma=False,
    )
```

```python
import functools

import jax
import jax.numpy as jnp
import ml_dtypes
import numpy as np
from jax import lax
from jax.experimental import pallas as pl
from jax.experimental.pallas import tpu as pltpu
from jax.sharding import PartitionSpec as P

MESH = pl.DeviceIdType.MESH
scale_lengths = (1.5, 4.0, 12.0)
scale_mix = (0.6, 0.5, 0.4)
NUM_LOADS = 12
bf16, f32 = jnp.bfloat16, jnp.float32


def gauss_table(length, spread):
    places = np.arange(length).astype(np.float32)
    offset = places[:, None] - places[None, :]
    norm_factor = np.sqrt(np.sqrt(np.float32(np.pi)) * np.float32(spread))
    values = np.exp(np.float32(-0.5) * offset * offset / np.float32(spread * spread)) / norm_factor
    values = np.where(np.abs(offset) <= 4.0 * spread, values, np.float32(0.0))
    return values.astype(ml_dtypes.bfloat16)


def row_table(table, blocks, levels):
    length = table.shape[0]
    rows = length // blocks
    wide = np.zeros((rows, blocks, levels, levels, length), ml_dtypes.bfloat16)
    by_row = table.reshape(blocks, rows, length).transpose(1, 0, 2)
    for level in range(levels):
        wide[:, :, level, level, :] = by_row
    return wide.reshape(rows * blocks * levels, levels * length)


def dot(a, b):
    return jnp.dot(a, b, preferred_element_type=f32)


def kernel(
    nw, nn,
    *refs,
):
    sources, out_ref = refs[:NUM_LOADS], refs[NUM_LOADS]
    loaded = refs[NUM_LOADS + 1 : 2 * NUM_LOADS + 1]
    (
        weights_ref, to_rows_ref, table_ref, column_ref, level_ref, vertical_ref,
        perturb_ref, flag_ref, value_ref, weight_ref, count_ref, to_levels_ref,
    ) = loaded
    (
        load_sem, send_a, recv_a, at_mine, at_all, send_b, recv_b, pick, pick_t, spread, vertical_t,
    send_sem, recv_sem, at_send_sem, at_recv_sem,
    ) = refs[2 * NUM_LOADS + 1 :]
    loads = [pltpu.make_async_copy(a, b, load_sem.at[n]) for n, (a, b) in enumerate(zip(sources, loaded))]
    for load in loads:
        load.start()

    me = lax.axis_index("wide")
    member = lax.axis_index("narrow")
    rows, blocks, levels, width = send_a.shape
    num_vars, num_levels, _ = vertical_ref.shape
    slot_rows = column_ref.shape[0]
    slots = slot_rows * 128
    cells = rows * width

    barrier = pltpu.get_barrier_semaphore()

    def greet(k, carry):
        peer = lax.rem(me + k, nw)
        pl.semaphore_signal(barrier, inc=1, device_id={"wide": peer}, device_id_type=MESH)
        return carry

    lax.fori_loop(1, nw, greet, 0)
    for k in range(1, nn):
        pl.semaphore_signal(
            barrier, inc=1, device_id={"narrow": lax.rem(member + k, nn)}, device_id_type=MESH
        )

    def exchange(source, target, phase):
        own = pltpu.make_async_copy(source.at[:, me], target.at[:, me], recv_sem.at[phase])
        own.start()

        def put(k, carry):
            peer = lax.rem(me + k, nw)
            pltpu.make_async_remote_copy(
                src_ref=source.at[:, peer],
                dst_ref=target.at[:, me],
                send_sem=send_sem.at[phase],
                recv_sem=recv_sem.at[phase],
                device_id={"wide": peer},
                device_id_type=MESH,
            ).start()
            return carry

        lax.fori_loop(1, nw, put, 0)

    def arrived(target, phase):
        pltpu.make_async_copy(target, target, recv_sem.at[phase]).wait()

    def departed(source, phase):
        part = source.at[:, pl.ds(0, nw - 1)]
        pltpu.make_async_copy(part, part, send_sem.at[phase]).wait()

    for load in loads[:3]:
        load.wait()

    own_weights = weights_ref[...]
    localized = None
    for s, mix in enumerate(scale_mix):
        across = dot(to_rows_ref[s], own_weights).astype(bf16)
        scaled = mix * dot(across, table_ref[s])
        localized = scaled if localized is None else localized + scaled
    send_a[...] = localized.astype(bf16).reshape(send_a.shape)
    pl.semaphore_wait(barrier, nw - 1 + nn - 1)
    exchange(send_a, recv_a, 0)

    for load in loads[3:6]:
        load.wait()

    cell_of = lax.broadcasted_iota(jnp.int32, (cells, 128), 0)
    cell_of_t = lax.broadcasted_iota(jnp.int32, (128, cells), 1)
    columns = column_ref[...]
    columns_t = jnp.transpose(columns)
    for r in range(slot_rows):
        part = slice(r * 128, (r + 1) * 128)
        pick[:, part] = jnp.where(cell_of == columns[r : r + 1, :], 1.0, 0.0).astype(bf16)
        pick_t[part, :] = jnp.where(cell_of_t == columns_t[:, r : r + 1], 1.0, 0.0).astype(bf16)
    for v in range(num_vars):
        vertical_t[v] = jnp.transpose(vertical_ref[v].astype(f32)).astype(bf16)

    for load in loads[6:]:
        load.wait()

    arrived(recv_a, 0)
    held = [recv_a[i].reshape(num_levels, width).astype(f32) for i in range(rows)]
    increment = []
    for v in range(num_vars):
        product = jnp.concatenate(
            [(perturb_ref[v * rows + i].astype(f32) * held[i]).astype(bf16) for i in range(rows)], axis=1
        )
        increment.append(dot(vertical_ref[v], product).astype(bf16))
    increment = jnp.concatenate(increment, axis=0)

    step = 256
    level_of = lax.broadcasted_iota(jnp.int32, (num_levels, 128), 0)
    for t in range(slots // step):
        met = dot(increment, pick[:, t * step : (t + 1) * step])
        for h in range(step // 128):
            r = t * (step // 128) + h
            here = level_of == level_ref[r : r + 1, :]
            for v in range(num_vars):
                block = met[v * num_levels : (v + 1) * num_levels, h * 128 : (h + 1) * 128]
                summed = jnp.sum(jnp.where(here, block, 0.0), axis=0, keepdims=True)
                at_mine[v, r : r + 1, :] = summed.astype(bf16)

    copies = []
    for k in range(1, nn):
        peer = lax.rem(member + k, nn)
        copy = pltpu.make_async_remote_copy(
            src_ref=at_mine,
            dst_ref=at_all.at[member],
            send_sem=at_send_sem,
            recv_sem=at_recv_sem,
            device_id={"narrow": peer},
            device_id_type=MESH,
        )
        copy.start()
        copies.append(copy)
    own = pltpu.make_async_copy(at_mine, at_all.at[member], at_recv_sem)
    own.start()
    pltpu.make_async_copy(at_all, at_all, at_recv_sem).wait()

    slot_of = lax.broadcasted_iota(jnp.int32, (slot_rows, 128), 0) * 128 + lax.broadcasted_iota(
        jnp.int32, (slot_rows, 128), 1
    )
    live = jnp.where((slot_of < count_ref[0]) & (flag_ref[...] > 0), 1.0, 0.0)
    for v in range(num_vars):
        at_obs = at_all[0, v].astype(f32)
        for k in range(1, nn):
            at_obs = at_obs + at_all[k, v].astype(f32)
        for r in range(slot_rows):
            part = slice(r * 128, (r + 1) * 128)
            misfit = jnp.where(
                live[r : r + 1] > 0.0,
                weight_ref[v : v + 1, part] * (at_obs[r : r + 1] - value_ref[v : v + 1, part]),
                0.0,
            )
            here = level_of == level_ref[r : r + 1, :]
            spread[v * num_levels : (v + 1) * num_levels, part] = jnp.where(here, misfit, 0.0).astype(bf16)
    adjoint = dot(spread[...], pick_t[...]).astype(bf16)

    sums = [None] * rows
    for v in range(num_vars):
        lifted = dot(vertical_t[v], adjoint[v * num_levels : (v + 1) * num_levels]).astype(bf16).astype(f32)
        for i in range(rows):
            term = perturb_ref[v * rows + i].astype(f32) * lifted[:, i * width : (i + 1) * width]
            sums[i] = term if sums[i] is None else sums[i] + term
    for i in range(rows):
        send_b[i] = sums[i].astype(bf16).reshape(send_b.shape[1:])
    exchange(send_b, recv_b, 1)
    arrived(recv_b, 1)

    level_grad = recv_b[...].reshape(rows * blocks * levels, width)
    gradient = own_weights.astype(f32)
    for s, mix in enumerate(scale_mix):
        back = dot(level_grad, table_ref[s]).astype(bf16)
        gradient = gradient + mix * dot(to_levels_ref[s], back)
    out_ref[...] = gradient

    departed(send_a, 0)
    departed(send_b, 1)
    pltpu.make_async_copy(at_all.at[pl.ds(0, nn - 1)], at_all.at[pl.ds(0, nn - 1)], at_send_sem).wait()


def solution(mesh):
    nw, nn = mesh.shape["wide"], mesh.shape["narrow"]

    def local(weights, perturb, vertical, obs_column, obs_level, obs_count, flag, obs_value, obs_weight):
        _, levels, length, width = weights.shape
        _, num_vars, rows, num_levels, _ = perturb.shape
        slots = obs_column.shape[0]
        slot_rows = slots // 128
        tables = [gauss_table(length, spread) for spread in scale_lengths]
        to_rows = np.stack([row_table(table, nw, levels) for table in tables])
        to_levels = np.ascontiguousarray(to_rows.transpose(0, 2, 1))
        operands = (
            weights.reshape(levels * length, width),
            jnp.asarray(to_rows),
            jnp.asarray(np.stack(tables)),
            obs_column.reshape(slot_rows, 128),
            obs_level.reshape(slot_rows, 128),
            vertical,
            perturb.reshape(num_vars * rows, num_levels, width),
            flag.reshape(slot_rows, 128),
            obs_value,
            obs_weight,
            obs_count,
            jnp.asarray(to_levels),
        )
        chunk = pltpu.VMEM((rows, nw, levels, width), bf16)
        vmem = pl.BlockSpec(memory_space=pltpu.VMEM)
        out = pl.pallas_call(
            functools.partial(kernel, nw, nn),
            out_shape=jax.ShapeDtypeStruct((levels * length, width), f32),
            in_specs=[pl.BlockSpec(memory_space=pltpu.HBM)] * NUM_LOADS,
            out_specs=vmem,
            scratch_shapes=[
                (pltpu.SMEM if operand is obs_count else pltpu.VMEM)(operand.shape, operand.dtype)
                for operand in operands
            ]
            + [
                pltpu.SemaphoreType.DMA((NUM_LOADS,)),
                chunk,
                chunk,
                pltpu.VMEM((num_vars, slot_rows, 128), bf16),
                pltpu.VMEM((nn, num_vars, slot_rows, 128), bf16),
                chunk,
                chunk,
                pltpu.VMEM((rows * width, slots), bf16),
                pltpu.VMEM((slots, rows * width), bf16),
                pltpu.VMEM((num_vars * num_levels, slots), bf16),
                pltpu.VMEM((num_vars, num_levels, num_levels), bf16),
                pltpu.SemaphoreType.DMA((2,)),
                pltpu.SemaphoreType.DMA((2,)),
                pltpu.SemaphoreType.DMA,
                pltpu.SemaphoreType.DMA,
            ],
            compiler_params=pltpu.CompilerParams(
                collective_id=0, has_side_effects=True, vmem_limit_bytes=60 * 1024 * 1024
            ),
        )(*operands)
        return out.reshape(weights.shape)

    placed = (
        P("narrow", "wide", None, None),
        P("narrow", None, "wide", None, None),
        P(),
        P("wide"),
        P("wide"),
        P("wide"),
        P("wide"),
        P(None, "wide"),
        P(None, "wide"),
    )
    return jax.shard_map(
        local,
        mesh=mesh,
        in_specs=placed,
        out_specs=P("narrow", "wide", None, None),
        check_vma=False,
    )
```

```python
import functools

import jax
import jax.numpy as jnp
import ml_dtypes
import numpy as np
from jax import lax
from jax.experimental import pallas as pl
from jax.experimental.pallas import tpu as pltpu
from jax.sharding import PartitionSpec as P

MESH = pl.DeviceIdType.MESH
scale_lengths = (1.5, 4.0, 12.0)
scale_mix = (0.6, 0.5, 0.4)
NUM_LOADS = 11
NARROW_FAR_FIRST = (6, 2, 5, 3, 4, 7, 1)
FAR_FIRST = sorted(range(1, 64), key=lambda k: -min(k, 64 - k))
bf16, f32 = jnp.bfloat16, jnp.float32


def gauss_table(length, spread):
    places = np.arange(length).astype(np.float32)
    offset = places[:, None] - places[None, :]
    norm_factor = np.sqrt(np.sqrt(np.float32(np.pi)) * np.float32(spread))
    values = np.exp(np.float32(-0.5) * offset * offset / np.float32(spread * spread)) / norm_factor
    values = np.where(np.abs(offset) <= 4.0 * spread, values, np.float32(0.0))
    return values.astype(ml_dtypes.bfloat16)


def row_table(table, blocks, levels):
    length = table.shape[0]
    rows = length // blocks
    wide = np.zeros((rows, blocks, levels, levels, length), ml_dtypes.bfloat16)
    by_row = table.reshape(blocks, rows, length).transpose(1, 0, 2)
    for level in range(levels):
        wide[:, :, level, level, :] = by_row
    return wide.reshape(rows * blocks * levels, levels * length)


def dot(a, b):
    return jnp.dot(a, b, preferred_element_type=f32)


def kernel(
    nw, nn,
    count_ref, *refs,
):
    sources, out_ref = refs[:NUM_LOADS], refs[NUM_LOADS]
    loaded = refs[NUM_LOADS + 1 : 2 * NUM_LOADS + 1]
    (
        weights_ref, to_rows_ref, table_ref, column_ref, level_ref, vertical_ref,
        perturb_ref, flag_ref, value_ref, weight_ref, to_levels_ref,
    ) = loaded
    (
        load_sem, send_a, recv_a, at_row, at_mine, at_all, send_b, recv_b, pick, pick_t, spread, vertical_t,
        at_level, value_rows, weight_rows,
    send_sem, recv_sem, at_send_sem, at_recv_sem,
    ) = refs[2 * NUM_LOADS + 1 :]
    me = lax.axis_index("wide")
    member = lax.axis_index("narrow")
    rows, blocks, levels, width = send_a.shape
    num_vars, num_levels, _ = vertical_ref.shape
    slot_rows = column_ref.shape[0]
    slots = slot_rows * 128
    cells = rows * width

    barrier = pltpu.get_barrier_semaphore()

    for far in FAR_FIRST:
        peer = lax.rem(me + far, nw)
        pl.semaphore_signal(barrier, inc=1, device_id={"wide": peer}, device_id_type=MESH)
    for k in range(1, nn):
        pl.semaphore_signal(
            barrier, inc=1, device_id={"narrow": lax.rem(member + k, nn)}, device_id_type=MESH
        )

    loads = [pltpu.make_async_copy(a, b, load_sem.at[n]) for n, (a, b) in enumerate(zip(sources, loaded))]
    for load in loads:
        load.start()

    def exchange(source, target, phase):
        own = pltpu.make_async_copy(source.at[:, me], target.at[:, me], recv_sem.at[phase])
        own.start()

        for far in FAR_FIRST:
            peer = lax.rem(me + far, nw)
            pltpu.make_async_remote_copy(
                src_ref=source.at[:, peer],
                dst_ref=target.at[:, me],
                send_sem=send_sem.at[phase],
                recv_sem=recv_sem.at[phase],
                device_id={"wide": peer},
                device_id_type=MESH,
            ).start()

    def arrived(target, phase):
        pltpu.make_async_copy(target, target, recv_sem.at[phase]).wait()

    def departed(source, phase):
        part = source.at[:, pl.ds(0, nw - 1)]
        pltpu.make_async_copy(part, part, send_sem.at[phase]).wait()

    for load in loads[:3]:
        load.wait()

    own_weights = weights_ref[...]
    localized = None
    for s, mix in enumerate(scale_mix):
        across = dot(to_rows_ref[s], own_weights).astype(bf16)
        scaled = mix * dot(across, table_ref[s])
        localized = scaled if localized is None else localized + scaled
    send_a[...] = localized.astype(bf16).reshape(send_a.shape)
    pl.semaphore_wait(barrier, nw - 1 + nn - 1)
    exchange(send_a, recv_a, 0)

    for load in loads[3:]:
        load.wait()

    cell_of = lax.broadcasted_iota(jnp.int32, (cells, 128), 0)
    cell_of_t = lax.broadcasted_iota(jnp.int32, (128, cells), 1)
    level_of = lax.broadcasted_iota(jnp.int32, (num_levels, 128), 0)
    columns = column_ref[...]
    columns_t = jnp.transpose(columns)
    slot_of = lax.broadcasted_iota(jnp.int32, (slot_rows, 128), 0) * 128 + lax.broadcasted_iota(
        jnp.int32, (slot_rows, 128), 1
    )
    live = (slot_of < count_ref[0]) & (flag_ref[...] > 0)
    for r in range(slot_rows):
        part = slice(r * 128, (r + 1) * 128)
        pick[:, part] = jnp.where(cell_of == columns[r : r + 1, :], 1.0, 0.0).astype(bf16)
        pick_t[part, :] = jnp.where(cell_of_t == columns_t[:, r : r + 1], 1.0, 0.0).astype(bf16)
        at_level[:, part] = jnp.where(level_of == level_ref[r : r + 1, :], 1.0, 0.0).astype(bf16)
        for v in range(num_vars):
            value_rows[v, r : r + 1, :] = value_ref[v : v + 1, part]
            weight_rows[v, r : r + 1, :] = weight_ref[v : v + 1, part]
    for v in range(num_vars):
        vertical_t[v] = jnp.transpose(vertical_ref[v].astype(f32)).astype(bf16)
        weight_rows[v] = jnp.where(live, weight_rows[v], 0.0)

    arrived(recv_a, 0)
    held = [recv_a[i].reshape(num_levels, width).astype(f32) for i in range(rows)]

    step = 256
    for v in range(num_vars):
        product = jnp.concatenate(
            [(perturb_ref[v * rows + i].astype(f32) * held[i]).astype(bf16) for i in range(rows)], axis=1
        )
        increment = dot(vertical_ref[v], product).astype(bf16)
        for t in range(slots // step):
            met = dot(increment, pick[:, t * step : (t + 1) * step])
            for h in range(step // 128):
                r = t * (step // 128) + h
                here = level_of == level_ref[r : r + 1, :]
                block = met[:, h * 128 : (h + 1) * 128]
                at_row[v, r : r + 1, :] = jnp.sum(jnp.where(here, block, 0.0), axis=0, keepdims=True)
        at_mine[v] = at_row[v].astype(bf16)
        pltpu.make_async_copy(at_mine.at[v], at_all.at[v, member], at_recv_sem.at[v]).start()
        for far in NARROW_FAR_FIRST:
            pltpu.make_async_remote_copy(
                src_ref=at_mine.at[v],
                dst_ref=at_all.at[v, member],
                send_sem=at_send_sem.at[v],
                recv_sem=at_recv_sem.at[v],
                device_id={"narrow": lax.rem(member + far, nn)},
                device_id_type=MESH,
            ).start()

    adjoint = []
    for v in range(num_vars):
        pltpu.make_async_copy(at_all.at[v], at_all.at[v], at_recv_sem.at[v]).wait()
        at_obs = at_all[v, 0].astype(f32)
        for k in range(1, nn):
            at_obs = at_obs + at_all[v, k].astype(f32)
        misfit = weight_rows[v] * (at_obs - value_rows[v])
        for r in range(slot_rows):
            part = slice(r * 128, (r + 1) * 128)
            row = jnp.broadcast_to(misfit[r : r + 1, :], (num_levels, 128)).astype(bf16)
            spread[v, :, part] = at_level[:, part] * row
        adjoint.append(dot(spread[v], pick_t[...]).astype(bf16))

    sums = [None] * rows
    for v in range(num_vars):
        lifted = dot(vertical_t[v], adjoint[v]).astype(bf16).astype(f32)
        for i in range(rows):
            term = perturb_ref[v * rows + i].astype(f32) * lifted[:, i * width : (i + 1) * width]
            sums[i] = term if sums[i] is None else sums[i] + term
    for i in range(rows):
        send_b[i] = sums[i].astype(bf16).reshape(send_b.shape[1:])
    exchange(send_b, recv_b, 1)
    arrived(recv_b, 1)

    level_grad = recv_b[...].reshape(rows * blocks * levels, width)
    gradient = own_weights.astype(f32)
    for s, mix in enumerate(scale_mix):
        back = dot(level_grad, table_ref[s]).astype(bf16)
        gradient = gradient + mix * dot(to_levels_ref[s], back)
    out_ref[...] = gradient

    departed(send_a, 0)
    departed(send_b, 1)
    for v in range(num_vars):
        part = at_all.at[v, pl.ds(0, nn - 1)]
        pltpu.make_async_copy(part, part, at_send_sem.at[v]).wait()


def solution(mesh):
    nw, nn = mesh.shape["wide"], mesh.shape["narrow"]

    def local(weights, perturb, vertical, obs_column, obs_level, obs_count, flag, obs_value, obs_weight):
        _, levels, length, width = weights.shape
        _, num_vars, rows, num_levels, _ = perturb.shape
        slots = obs_column.shape[0]
        slot_rows = slots // 128
        tables = [gauss_table(length, spread) for spread in scale_lengths]
        to_rows = np.stack([row_table(table, nw, levels) for table in tables])
        to_levels = np.ascontiguousarray(to_rows.transpose(0, 2, 1))
        operands = (
            weights.reshape(levels * length, width),
            jnp.asarray(to_rows),
            jnp.asarray(np.stack(tables)),
            obs_column.reshape(slot_rows, 128),
            obs_level.reshape(slot_rows, 128),
            vertical,
            perturb.reshape(num_vars * rows, num_levels, width),
            flag.reshape(slot_rows, 128),
            obs_value,
            obs_weight,
            jnp.asarray(to_levels),
        )
        chunk = pltpu.VMEM((rows, nw, levels, width), bf16)
        vmem = pl.BlockSpec(memory_space=pltpu.VMEM)
        out = pl.pallas_call(
            functools.partial(kernel, nw, nn),
            out_shape=pltpu.VMEM((levels * length, width), f32),
            in_specs=[pl.BlockSpec(memory_space=pltpu.SMEM)] + [pl.BlockSpec(memory_space=pltpu.HBM)] * NUM_LOADS,
            out_specs=vmem,
            scratch_shapes=[pltpu.VMEM(operand.shape, operand.dtype) for operand in operands]
            + [
                pltpu.SemaphoreType.DMA((NUM_LOADS,)),
                chunk,
                chunk,
                pltpu.VMEM((num_vars, slot_rows, 128), f32),
                pltpu.VMEM((num_vars, slot_rows, 128), bf16),
                pltpu.VMEM((num_vars, nn, slot_rows, 128), bf16),
                chunk,
                chunk,
                pltpu.VMEM((rows * width, slots), bf16),
                pltpu.VMEM((slots, rows * width), bf16),
                pltpu.VMEM((num_vars, num_levels, slots), bf16),
                pltpu.VMEM((num_vars, num_levels, num_levels), bf16),
                pltpu.VMEM((num_levels, slots), bf16),
                pltpu.VMEM((num_vars, slot_rows, 128), f32),
                pltpu.VMEM((num_vars, slot_rows, 128), f32),
                pltpu.SemaphoreType.DMA((2,)),
                pltpu.SemaphoreType.DMA((2,)),
                pltpu.SemaphoreType.DMA((num_vars,)),
                pltpu.SemaphoreType.DMA((num_vars,)),
            ],
            compiler_params=pltpu.CompilerParams(
                collective_id=0, has_side_effects=True, vmem_limit_bytes=32 * 1024 * 1024
            ),
        )(
            obs_count,
            *(
                pltpu.with_memory_space_constraint(operand, pltpu.HBM)
                for operand in operands
            )
        )
        return out.reshape(weights.shape)

    placed = (
        P("narrow", "wide", None, None),
        P("narrow", None, "wide", None, None),
        P(),
        P("wide"),
        P("wide"),
        P("wide"),
        P("wide"),
        P(None, "wide"),
        P(None, "wide"),
    )
    return jax.shard_map(
        local,
        mesh=mesh,
        in_specs=placed,
        out_specs=P("narrow", "wide", None, None),
        check_vma=False,
    )
```

```python
import functools

import jax
import jax.numpy as jnp
import ml_dtypes
import numpy as np
from jax import lax
from jax.experimental import pallas as pl
from jax.experimental.pallas import tpu as pltpu
from jax.sharding import PartitionSpec as P

MESH = pl.DeviceIdType.MESH
scale_lengths = (1.5, 4.0, 12.0)
scale_mix = (0.6, 0.5, 0.4)
NUM_LOADS = 11
NARROW_FAR_FIRST = (6, 2, 5, 3, 4, 7, 1)
FAR_FIRST = sorted(range(1, 64), key=lambda k: -min(k, 64 - k))
bf16, f32 = jnp.bfloat16, jnp.float32


def gauss_table(length, spread):
    places = np.arange(length).astype(np.float32)
    offset = places[:, None] - places[None, :]
    norm_factor = np.sqrt(np.sqrt(np.float32(np.pi)) * np.float32(spread))
    values = np.exp(np.float32(-0.5) * offset * offset / np.float32(spread * spread)) / norm_factor
    values = np.where(np.abs(offset) <= 4.0 * spread, values, np.float32(0.0))
    return values.astype(ml_dtypes.bfloat16)


def row_table(table, blocks, levels):
    length = table.shape[0]
    rows = length // blocks
    wide = np.zeros((blocks, rows, levels, levels, length), ml_dtypes.bfloat16)
    by_row = table.reshape(blocks, rows, length)
    for level in range(levels):
        wide[:, :, level, level, :] = by_row
    return wide.reshape(rows * blocks * levels, levels * length)


def dot(a, b):
    return jnp.dot(a, b, preferred_element_type=f32)


def kernel(
    nw, nn,
    count_ref, *refs,
):
    sources, out_ref = refs[:NUM_LOADS], refs[NUM_LOADS]
    loaded = refs[NUM_LOADS + 1 : 2 * NUM_LOADS + 1]
    (
        weights_ref, to_rows_ref, table_ref, column_ref, level_ref, vertical_ref,
        perturb_ref, flag_ref, value_ref, weight_ref, to_levels_ref,
    ) = loaded
    (
        load_sem, send_a, recv_a, at_row, at_mine, at_all, send_b, recv_b, pick, pick_t, spread, vertical_t,
        at_level, lift, lift_low, value_rows, weight_rows,
    send_sem, recv_sem, at_send_sem, at_recv_sem,
    ) = refs[2 * NUM_LOADS + 1 :]
    me = lax.axis_index("wide")
    member = lax.axis_index("narrow")
    blocks, rows, levels, width = send_a.shape
    num_vars, num_levels, _ = vertical_ref.shape
    slot_rows = column_ref.shape[0]
    slots = slot_rows * 128
    cells = rows * width

    barrier = pltpu.get_barrier_semaphore()

    for far in FAR_FIRST:
        peer = lax.rem(me + far, nw)
        pl.semaphore_signal(barrier, inc=1, device_id={"wide": peer}, device_id_type=MESH)
    for k in range(1, nn):
        pl.semaphore_signal(
            barrier, inc=1, device_id={"narrow": lax.rem(member + k, nn)}, device_id_type=MESH
        )

    loads = [pltpu.make_async_copy(a, b, load_sem.at[n]) for n, (a, b) in enumerate(zip(sources, loaded))]
    for load in loads:
        load.start()

    def exchange(source, target, phase):
        own = pltpu.make_async_copy(source.at[me], target.at[me], recv_sem.at[phase])
        own.start()

        for far in FAR_FIRST:
            peer = lax.rem(me + far, nw)
            pltpu.make_async_remote_copy(
                src_ref=source.at[peer],
                dst_ref=target.at[me],
                send_sem=send_sem.at[phase],
                recv_sem=recv_sem.at[phase],
                device_id={"wide": peer},
                device_id_type=MESH,
            ).start()

    def arrived(target, phase):
        pltpu.make_async_copy(target, target, recv_sem.at[phase]).wait()

    def departed(source, phase):
        part = source.at[pl.ds(0, nw - 1)]
        pltpu.make_async_copy(part, part, send_sem.at[phase]).wait()

    for load in loads[:3]:
        load.wait()

    own_weights = weights_ref[...]
    localized = None
    for s, mix in enumerate(scale_mix):
        across = dot(to_rows_ref[s], own_weights).astype(bf16)
        scaled = mix * dot(across, table_ref[s])
        localized = scaled if localized is None else localized + scaled
    send_a[...] = localized.astype(bf16).reshape(send_a.shape)
    pl.semaphore_wait(barrier, nw - 1 + nn - 1)
    exchange(send_a, recv_a, 0)

    for load in loads[3:]:
        load.wait()

    cell_of = lax.broadcasted_iota(jnp.int32, (cells, 128), 0)
    cell_of_t = lax.broadcasted_iota(jnp.int32, (128, cells), 1)
    level_of = lax.broadcasted_iota(jnp.int32, (num_levels, 128), 0)
    columns = column_ref[...]
    columns_t = jnp.transpose(columns)
    slot_of = lax.broadcasted_iota(jnp.int32, (slot_rows, 128), 0) * 128 + lax.broadcasted_iota(
        jnp.int32, (slot_rows, 128), 1
    )
    live = (slot_of < count_ref[0]) & (flag_ref[...] > 0)
    for r in range(slot_rows):
        part = slice(r * 128, (r + 1) * 128)
        pick[:, part] = jnp.where(cell_of == columns[r : r + 1, :], 1.0, 0.0).astype(bf16)
        pick_t[part, :] = jnp.where(cell_of_t == columns_t[:, r : r + 1], 1.0, 0.0).astype(bf16)
        at_level[:, part] = jnp.where(level_of == level_ref[r : r + 1, :], 1.0, 0.0).astype(bf16)
        for v in range(num_vars):
            value_rows[v, r : r + 1, :] = value_ref[v : v + 1, part]
            weight_rows[v, r : r + 1, :] = weight_ref[v : v + 1, part]
    for v in range(num_vars):
        vertical_t[v] = jnp.transpose(vertical_ref[v].astype(f32)).astype(bf16)
        weight_rows[v] = jnp.where(live, weight_rows[v], 0.0)
    step = 256
    for v in range(num_vars):
        for t in range(slots // step):
            part = slice(t * step, (t + 1) * step)
            rows_of = dot(vertical_t[v], at_level[:, part])
            lift[v, :, part] = rows_of
            lift_low[v, :, part] = rows_of.astype(bf16)

    arrived(recv_a, 0)
    held = [recv_a[:, i].reshape(num_levels, width).astype(f32) for i in range(rows)]

    for v in range(num_vars):
        product = jnp.concatenate(
            [(perturb_ref[v * rows + i].astype(f32) * held[i]).astype(bf16) for i in range(rows)], axis=1
        )
        for t in range(slots // step):
            met = dot(product, pick[:, t * step : (t + 1) * step])
            for h in range(step // 128):
                r = t * (step // 128) + h
                block = met[:, h * 128 : (h + 1) * 128] * lift[v, :, r * 128 : (r + 1) * 128]
                at_row[v, r : r + 1, :] = jnp.sum(block, axis=0, keepdims=True)
        at_mine[v] = at_row[v].astype(bf16)
        pltpu.make_async_copy(at_mine.at[v], at_all.at[v, member], at_recv_sem.at[v]).start()
        for far in NARROW_FAR_FIRST:
            pltpu.make_async_remote_copy(
                src_ref=at_mine.at[v],
                dst_ref=at_all.at[v, member],
                send_sem=at_send_sem.at[v],
                recv_sem=at_recv_sem.at[v],
                device_id={"narrow": lax.rem(member + far, nn)},
                device_id_type=MESH,
            ).start()

    sums = [None] * rows
    for v in range(num_vars):
        pltpu.make_async_copy(at_all.at[v], at_all.at[v], at_recv_sem.at[v]).wait()
        at_obs = at_all[v, 0].astype(f32)
        for k in range(1, nn):
            at_obs = at_obs + at_all[v, k].astype(f32)
        misfit = weight_rows[v] * (at_obs - value_rows[v])
        for r in range(slot_rows):
            part = slice(r * 128, (r + 1) * 128)
            row = jnp.broadcast_to(misfit[r : r + 1, :], (num_levels, 128)).astype(bf16)
            spread[v, :, part] = lift_low[v, :, part] * row
        lifted = dot(spread[v], pick_t[...]).astype(bf16).astype(f32)
        for i in range(rows):
            term = perturb_ref[v * rows + i].astype(f32) * lifted[:, i * width : (i + 1) * width]
            sums[i] = term if sums[i] is None else sums[i] + term
    for i in range(rows):
        send_b[:, i] = sums[i].astype(bf16).reshape(blocks, levels, width)
    exchange(send_b, recv_b, 1)
    arrived(recv_b, 1)

    level_grad = recv_b[...].reshape(rows * blocks * levels, width)
    back = [(mix * dot(level_grad, table_ref[s])).astype(bf16) for s, mix in enumerate(scale_mix)]
    gradient = own_weights.astype(f32) + dot(to_levels_ref[...], jnp.concatenate(back, axis=0))
    out_ref[...] = gradient

    departed(send_a, 0)
    departed(send_b, 1)
    for v in range(num_vars):
        part = at_all.at[v, pl.ds(0, nn - 1)]
        pltpu.make_async_copy(part, part, at_send_sem.at[v]).wait()


def solution(mesh):
    nw, nn = mesh.shape["wide"], mesh.shape["narrow"]

    def local(weights, perturb, vertical, obs_column, obs_level, obs_count, flag, obs_value, obs_weight):
        _, levels, length, width = weights.shape
        _, num_vars, rows, num_levels, _ = perturb.shape
        slots = obs_column.shape[0]
        slot_rows = slots // 128
        tables = [gauss_table(length, spread) for spread in scale_lengths]
        to_rows = np.stack([row_table(table, nw, levels) for table in tables])
        to_levels = np.concatenate(list(to_rows.transpose(0, 2, 1)), axis=1)
        operands = (
            weights.reshape(levels * length, width),
            jnp.asarray(to_rows),
            jnp.asarray(np.stack(tables)),
            obs_column.reshape(slot_rows, 128),
            obs_level.reshape(slot_rows, 128),
            vertical,
            perturb.reshape(num_vars * rows, num_levels, width),
            flag.reshape(slot_rows, 128),
            obs_value,
            obs_weight,
            jnp.asarray(to_levels),
        )
        chunk = pltpu.VMEM((nw, rows, levels, width), bf16)
        vmem = pl.BlockSpec(memory_space=pltpu.VMEM)
        out = pl.pallas_call(
            functools.partial(kernel, nw, nn),
            out_shape=pltpu.VMEM((levels * length, width), f32),
            in_specs=[pl.BlockSpec(memory_space=pltpu.SMEM)] + [pl.BlockSpec(memory_space=pltpu.HBM)] * NUM_LOADS,
            out_specs=vmem,
            scratch_shapes=[pltpu.VMEM(operand.shape, operand.dtype) for operand in operands]
            + [
                pltpu.SemaphoreType.DMA((NUM_LOADS,)),
                chunk,
                chunk,
                pltpu.VMEM((num_vars, slot_rows, 128), f32),
                pltpu.VMEM((num_vars, slot_rows, 128), bf16),
                pltpu.VMEM((num_vars, nn, slot_rows, 128), bf16),
                chunk,
                chunk,
                pltpu.VMEM((rows * width, slots), bf16),
                pltpu.VMEM((slots, rows * width), bf16),
                pltpu.VMEM((num_vars, num_levels, slots), bf16),
                pltpu.VMEM((num_vars, num_levels, num_levels), bf16),
                pltpu.VMEM((num_levels, slots), bf16),
                pltpu.VMEM((num_vars, num_levels, slots), f32),
                pltpu.VMEM((num_vars, num_levels, slots), bf16),
                pltpu.VMEM((num_vars, slot_rows, 128), f32),
                pltpu.VMEM((num_vars, slot_rows, 128), f32),
                pltpu.SemaphoreType.DMA((2,)),
                pltpu.SemaphoreType.DMA((2,)),
                pltpu.SemaphoreType.DMA((num_vars,)),
                pltpu.SemaphoreType.DMA((num_vars,)),
            ],
            compiler_params=pltpu.CompilerParams(
                collective_id=0, has_side_effects=True, vmem_limit_bytes=32 * 1024 * 1024
            ),
        )(
            obs_count,
            *(
                pltpu.with_memory_space_constraint(operand, pltpu.HBM)
                for operand in operands
            )
        )
        return out.reshape(weights.shape)

    placed = (
        P("narrow", "wide", None, None),
        P("narrow", None, "wide", None, None),
        P(),
        P("wide"),
        P("wide"),
        P("wide"),
        P("wide"),
        P(None, "wide"),
        P(None, "wide"),
    )
    return jax.shard_map(
        local,
        mesh=mesh,
        in_specs=placed,
        out_specs=P("narrow", "wide", None, None),
        check_vma=False,
    )
```

```python
import functools

import jax
import jax.numpy as jnp
import ml_dtypes
import numpy as np
from jax import lax
from jax.experimental import pallas as pl
from jax.experimental.pallas import tpu as pltpu
from jax.sharding import PartitionSpec as P

MESH = pl.DeviceIdType.MESH
scale_lengths = (1.5, 4.0, 12.0)
scale_mix = (0.6, 0.5, 0.4)
NUM_LOADS = 11
NARROW_FAR_FIRST = (6, 2, 5, 3, 4, 7, 1)
FAR_FIRST = sorted(range(1, 64), key=lambda k: -min(k, 64 - k))
bf16, f32 = jnp.bfloat16, jnp.float32


def gauss_table(length, spread):
    places = np.arange(length).astype(np.float32)
    offset = places[:, None] - places[None, :]
    norm_factor = np.sqrt(np.sqrt(np.float32(np.pi)) * np.float32(spread))
    values = np.exp(np.float32(-0.5) * offset * offset / np.float32(spread * spread)) / norm_factor
    values = np.where(np.abs(offset) <= 4.0 * spread, values, np.float32(0.0))
    return values.astype(ml_dtypes.bfloat16)


def row_table(table, blocks, levels):
    length = table.shape[0]
    rows = length // blocks
    wide = np.zeros((blocks, rows, levels, levels, length), ml_dtypes.bfloat16)
    by_row = table.reshape(blocks, rows, length)
    for level in range(levels):
        wide[:, :, level, level, :] = by_row
    return wide.reshape(rows * blocks * levels, levels * length)


def wrap(index, count):
    return jnp.where(index >= count, index - count, index)


def dot(a, b):
    return jnp.dot(a, b, preferred_element_type=f32)


def kernel(
    nw, nn,
    count_ref, *refs,
):
    sources, out_ref = refs[:NUM_LOADS], refs[NUM_LOADS]
    loaded = refs[NUM_LOADS + 1 : 2 * NUM_LOADS + 1]
    (
        weights_ref, to_rows_ref, table_ref, column_ref, level_ref, vertical_ref,
        perturb_ref, flag_ref, value_ref, weight_ref, to_levels_ref,
    ) = loaded
    (
        load_sem, send_a, recv_a, at_row, at_mine, at_all, send_b, recv_b, pick, pick_t, spread, vertical_t,
        at_level, lift, lift_low, value_rows, weight_rows,
    send_sem, recv_sem, at_send_sem, at_recv_sem,
    ) = refs[2 * NUM_LOADS + 1 :]
    me = lax.axis_index("wide")
    member = lax.axis_index("narrow")
    blocks, rows, levels, width = send_a.shape
    num_vars, num_levels, _ = vertical_ref.shape
    slot_rows = column_ref.shape[0]
    slots = slot_rows * 128
    cells = rows * width

    barrier = pltpu.get_barrier_semaphore()

    for far in FAR_FIRST:
        peer = wrap(me + far, nw)
        pl.semaphore_signal(barrier, inc=1, device_id={"wide": peer}, device_id_type=MESH)
    for k in range(1, nn):
        pl.semaphore_signal(
            barrier, inc=1, device_id={"narrow": lax.rem(member + k, nn)}, device_id_type=MESH
        )

    loads = [pltpu.make_async_copy(a, b, load_sem.at[n]) for n, (a, b) in enumerate(zip(sources, loaded))]
    for load in loads:
        load.start()

    def exchange(source, target, phase):
        for far in FAR_FIRST:
            peer = wrap(me + far, nw)
            pltpu.make_async_remote_copy(
                src_ref=source.at[peer],
                dst_ref=target.at[me],
                send_sem=send_sem.at[phase],
                recv_sem=recv_sem.at[phase],
                device_id={"wide": peer},
                device_id_type=MESH,
            ).start()
        pltpu.make_async_copy(source.at[me], target.at[me], recv_sem.at[phase]).start()

    def arrived(target, phase):
        pltpu.make_async_copy(target, target, recv_sem.at[phase]).wait()

    def departed(source, phase):
        part = source.at[pl.ds(0, nw - 1)]
        pltpu.make_async_copy(part, part, send_sem.at[phase]).wait()

    for load in loads[:3]:
        load.wait()

    own_weights = weights_ref[...]
    localized = None
    for s, mix in enumerate(scale_mix):
        across = dot(to_rows_ref[s], own_weights).astype(bf16)
        scaled = mix * dot(across, table_ref[s])
        localized = scaled if localized is None else localized + scaled
    send_a[...] = localized.astype(bf16).reshape(send_a.shape)
    pl.semaphore_wait(barrier, nw - 1 + nn - 1)
    exchange(send_a, recv_a, 0)

    for load in loads[3:]:
        load.wait()

    cell_of = lax.broadcasted_iota(jnp.int32, (cells, 128), 0)
    cell_of_t = lax.broadcasted_iota(jnp.int32, (128, cells), 1)
    level_of = lax.broadcasted_iota(jnp.int32, (num_levels, 128), 0)
    columns = column_ref[...]
    columns_t = jnp.transpose(columns)
    slot_of = lax.broadcasted_iota(jnp.int32, (slot_rows, 128), 0) * 128 + lax.broadcasted_iota(
        jnp.int32, (slot_rows, 128), 1
    )
    live = (slot_of < count_ref[0]) & (flag_ref[...] > 0)
    for r in range(slot_rows):
        part = slice(r * 128, (r + 1) * 128)
        pick[:, part] = jnp.where(cell_of == columns[r : r + 1, :], 1.0, 0.0).astype(bf16)
        pick_t[part, :] = jnp.where(cell_of_t == columns_t[:, r : r + 1], 1.0, 0.0).astype(bf16)
        at_level[:, part] = jnp.where(level_of == level_ref[r : r + 1, :], 1.0, 0.0).astype(bf16)
        for v in range(num_vars):
            value_rows[v, r : r + 1, :] = value_ref[v : v + 1, part]
            weight_rows[v, r : r + 1, :] = weight_ref[v : v + 1, part]
    for v in range(num_vars):
        vertical_t[v] = jnp.transpose(vertical_ref[v].astype(f32)).astype(bf16)
        weight_rows[v] = jnp.where(live, weight_rows[v], 0.0)
    step = 256
    for v in range(num_vars):
        for t in range(slots // step):
            part = slice(t * step, (t + 1) * step)
            rows_of = dot(vertical_t[v], at_level[:, part])
            lift[v, :, part] = rows_of
            lift_low[v, :, part] = rows_of.astype(bf16)

    arrived(recv_a, 0)
    held = [recv_a[:, i].reshape(num_levels, width).astype(f32) for i in range(rows)]

    for v in range(num_vars):
        product = jnp.concatenate(
            [(perturb_ref[v * rows + i].astype(f32) * held[i]).astype(bf16) for i in range(rows)], axis=1
        )
        met_rows = []
        for t in range(slots // step):
            met = dot(product, pick[:, t * step : (t + 1) * step])
            for h in range(step // 128):
                r = t * (step // 128) + h
                block = met[:, h * 128 : (h + 1) * 128] * lift[v, :, r * 128 : (r + 1) * 128]
                met_rows.append(jnp.sum(block, axis=0, keepdims=True))
        at_mine[v] = jnp.concatenate(met_rows, axis=0).astype(bf16)
        for far in NARROW_FAR_FIRST:
            pltpu.make_async_remote_copy(
                src_ref=at_mine.at[v],
                dst_ref=at_all.at[v, member],
                send_sem=at_send_sem.at[v],
                recv_sem=at_recv_sem.at[v],
                device_id={"narrow": lax.rem(member + far, nn)},
                device_id_type=MESH,
            ).start()
        pltpu.make_async_copy(at_mine.at[v], at_all.at[v, member], at_recv_sem.at[v]).start()

    sums = [None] * rows
    for v in range(num_vars):
        pltpu.make_async_copy(at_all.at[v], at_all.at[v], at_recv_sem.at[v]).wait()
        at_obs = at_all[v, 0].astype(f32)
        for k in range(1, nn):
            at_obs = at_obs + at_all[v, k].astype(f32)
        misfit = weight_rows[v] * (at_obs - value_rows[v])
        for r in range(slot_rows):
            part = slice(r * 128, (r + 1) * 128)
            row = jnp.broadcast_to(misfit[r : r + 1, :], (num_levels, 128)).astype(bf16)
            spread[v, :, part] = lift_low[v, :, part] * row
        lifted = dot(spread[v], pick_t[...]).astype(bf16).astype(f32)
        for i in range(rows):
            term = perturb_ref[v * rows + i].astype(f32) * lifted[:, i * width : (i + 1) * width]
            sums[i] = term if sums[i] is None else sums[i] + term
    for i in range(rows):
        send_b[:, i] = sums[i].astype(bf16).reshape(blocks, levels, width)
    exchange(send_b, recv_b, 1)
    arrived(recv_b, 1)

    level_grad = recv_b[...].reshape(rows * blocks * levels, width)
    back = [(mix * dot(level_grad, table_ref[s])).astype(bf16) for s, mix in enumerate(scale_mix)]
    gradient = own_weights.astype(f32) + dot(to_levels_ref[...], jnp.concatenate(back, axis=0))
    out_ref[...] = gradient

    departed(send_a, 0)
    departed(send_b, 1)
    for v in range(num_vars):
        part = at_all.at[v, pl.ds(0, nn - 1)]
        pltpu.make_async_copy(part, part, at_send_sem.at[v]).wait()


def solution(mesh):
    nw, nn = mesh.shape["wide"], mesh.shape["narrow"]

    def local(weights, perturb, vertical, obs_column, obs_level, obs_count, flag, obs_value, obs_weight):
        _, levels, length, width = weights.shape
        _, num_vars, rows, num_levels, _ = perturb.shape
        slots = obs_column.shape[0]
        slot_rows = slots // 128
        tables = [gauss_table(length, spread) for spread in scale_lengths]
        to_rows = np.stack([row_table(table, nw, levels) for table in tables])
        to_levels = np.concatenate(list(to_rows.transpose(0, 2, 1)), axis=1)
        operands = (
            weights.reshape(levels * length, width),
            jnp.asarray(to_rows),
            jnp.asarray(np.stack(tables)),
            obs_column.reshape(slot_rows, 128),
            obs_level.reshape(slot_rows, 128),
            vertical,
            perturb.reshape(num_vars * rows, num_levels, width),
            flag.reshape(slot_rows, 128),
            obs_value,
            obs_weight,
            jnp.asarray(to_levels),
        )
        chunk = pltpu.VMEM((nw, rows, levels, width), bf16)
        vmem = pl.BlockSpec(memory_space=pltpu.VMEM)
        out = pl.pallas_call(
            functools.partial(kernel, nw, nn),
            out_shape=pltpu.VMEM((levels * length, width), f32),
            in_specs=[pl.BlockSpec(memory_space=pltpu.SMEM)] + [pl.BlockSpec(memory_space=pltpu.HBM)] * NUM_LOADS,
            out_specs=vmem,
            scratch_shapes=[pltpu.VMEM(operand.shape, operand.dtype) for operand in operands]
            + [
                pltpu.SemaphoreType.DMA((NUM_LOADS,)),
                chunk,
                chunk,
                pltpu.VMEM((num_vars, slot_rows, 128), f32),
                pltpu.VMEM((num_vars, slot_rows, 128), bf16),
                pltpu.VMEM((num_vars, nn, slot_rows, 128), bf16),
                chunk,
                chunk,
                pltpu.VMEM((rows * width, slots), bf16),
                pltpu.VMEM((slots, rows * width), bf16),
                pltpu.VMEM((num_vars, num_levels, slots), bf16),
                pltpu.VMEM((num_vars, num_levels, num_levels), bf16),
                pltpu.VMEM((num_levels, slots), bf16),
                pltpu.VMEM((num_vars, num_levels, slots), f32),
                pltpu.VMEM((num_vars, num_levels, slots), bf16),
                pltpu.VMEM((num_vars, slot_rows, 128), f32),
                pltpu.VMEM((num_vars, slot_rows, 128), f32),
                pltpu.SemaphoreType.DMA((2,)),
                pltpu.SemaphoreType.DMA((2,)),
                pltpu.SemaphoreType.DMA((num_vars,)),
                pltpu.SemaphoreType.DMA((num_vars,)),
            ],
            compiler_params=pltpu.CompilerParams(
                collective_id=0, has_side_effects=True, vmem_limit_bytes=32 * 1024 * 1024
            ),
        )(
            obs_count,
            *(
                pltpu.with_memory_space_constraint(operand, pltpu.HBM)
                for operand in operands
            )
        )
        return out.reshape(weights.shape)

    placed = (
        P("narrow", "wide", None, None),
        P("narrow", None, "wide", None, None),
        P(),
        P("wide"),
        P("wide"),
        P("wide"),
        P("wide"),
        P(None, "wide"),
        P(None, "wide"),
    )
    return jax.shard_map(
        local,
        mesh=mesh,
        in_specs=placed,
        out_specs=P("narrow", "wide", None, None),
        check_vma=False,
    )
```
